128 devices in a mesh: dp: 32 (over x_lo, z, y), proj: 4 (over x_hi, core).
Axes of the slice: x: 4 (x_hi: 2, x_lo: 2; x = x_hi * 2 + x_lo), y: 4, z: 4, core: 2. Of those that a mesh axis runs over, the one named last changes fastest.
Arguments:
- train_hidden: bfloat16 [8192, 8, 11008], P('dp', None, 'proj'), may hold values from -6 to 6
- train_cotangent: bfloat16 [8192, 8, 4096], P('dp', None, 'proj'), may hold values from -6 to 6
- test_hidden: bfloat16 [4096, 8, 11008], P('dp', None, 'proj'), may hold values from -6 to 6
- test_cotangent: bfloat16 [4096, 8, 4096], P('dp', None, 'proj'), may hold values from -6 to 6
- proj_hidden: bfloat16 [11008, 32], P('proj'), may hold values from -0.0546875 to 0.0546875
- proj_cotangent: bfloat16 [4096, 64], P('proj'), may hold values from -0.09375 to 0.09375
- train_lengths: int32 [8192], P('dp'), may hold values from 1 to 8, as said below
- test_lengths: int32 [4096], P('dp'), may hold values from 1 to 8, as said below
Outputs:
- scores: float32 [8192, 4096], P(('dp', 'proj'))
The draws below stay inside these ranges and needn't reach their ends.
Inputs may be any that keep to these rules, and one draw needn't show every extreme that they name: `train_lengths`: each example's count of valid tokens; the first example of every set has all 8. `test_lengths`: each example's count of valid tokens; the first example of every set has all 8.
All inputs are finite; a program needn't handle non-finite values.
Results may differ from the reference program's by a relative error of at most 0.029.
Values may be sent and summed in bfloat16 or wider, within the bound.
No kernel may reach another device: no remote copies, remote signals or barrier semaphores. Data moves between devices by JAX's collectives and lax.ppermute only.
A program may use at most 256 MiB of HBM per device.

```python
import math
import jax
import jax.numpy as jnp
from jax import lax

D = 4096
FF = 11008
KX = 32
KG = 64
K = 2048
TOKS = 8
N_TRAIN = 8192
N_TEST = 4096


def draw_train_lengths(key, part):
    key = jax.random.fold_in(key, 11)
    drawn = jax.random.randint(key, (N_TRAIN,), 1, TOKS + 1)
    return drawn.at[0].set(TOKS).astype(jnp.int32)


def draw_test_lengths(key, part):
    key = jax.random.fold_in(key, 23)
    drawn = jax.random.randint(key, (N_TEST,), 1, TOKS + 1)
    return drawn.at[0].set(TOKS).astype(jnp.int32)


def steps_of(rng, dims, shards, least, high):
    gain, own = 1.0, jax.random.fold_in(rng, 6)
    for dim, shards_of in shards:
        draws = jnp.exp(jax.random.uniform(jax.random.fold_in(own, dim), (shards_of,), jnp.float32, least / len(shards), high / len(shards)))
        gain = gain * jnp.repeat(draws, dims[dim] // shards_of).reshape([-1 if axis == dim else 1 for axis in range(len(dims))])
    return gain


def normal_values(rng, shape, scale, limit, shards=(), held_as=jnp.bfloat16):
    entries = scale * jax.random.normal(rng, shape, jnp.float32)
    if shards:
        entries = entries * steps_of(rng, shape, shards, -0.22, 0.18)
    return jnp.clip(entries, -limit, limit).astype(held_as)


def setup_inputs(seed: int = 0) -> dict:
    keys = jax.random.split(jax.random.key(seed), 9)
    return {
        "train_hidden": normal_values(keys[0], (N_TRAIN, TOKS, FF), 1.0, 6.0, ((0, 32), (2, 4))),
        "train_cotangent": normal_values(keys[1], (N_TRAIN, TOKS, D), 1.0, 6.0, ((0, 32), (2, 4))),
        "test_hidden": normal_values(keys[2], (N_TEST, TOKS, FF), 1.0, 6.0, ((0, 32), (2, 4))),
        "test_cotangent": normal_values(keys[3], (N_TEST, TOKS, D), 1.0, 6.0, ((0, 32), (2, 4))),
        "proj_hidden": normal_values(keys[4], (FF, KX), FF ** -0.5, 0.0546875, ((0, 4),)),
        "proj_cotangent": normal_values(keys[5], (D, KG), D ** -0.5, 0.09375, ((0, 4),)),
        "train_lengths": draw_train_lengths(jax.random.fold_in(keys[8], 71), 0),
        "test_lengths": draw_test_lengths(jax.random.fold_in(keys[8], 71), 0),
    }


def features_of(hidden, cotangent, proj_hidden, proj_cotangent, lengths):
    count = hidden.shape[0]
    toks = hidden.shape[1]
    left = jnp.dot(hidden.reshape(count * toks, FF).astype(jnp.float32), proj_hidden.astype(jnp.float32), preferred_element_type=jnp.float32).reshape(count, toks, KX)
    right = jnp.dot(cotangent.reshape(count * toks, D).astype(jnp.float32), proj_cotangent.astype(jnp.float32), preferred_element_type=jnp.float32).reshape(count, toks, KG)
    valid = (jnp.arange(toks, dtype=jnp.int32)[None, :] < lengths[:, None]).astype(jnp.float32)
    left = left * valid[:, :, None]
    outer = jnp.einsum('nsb,nsa->nba', right, left)
    return outer.reshape(count, KG * KX).astype(jnp.bfloat16)

def reference(train_hidden, train_cotangent, test_hidden, test_cotangent, proj_hidden, proj_cotangent, train_lengths, test_lengths):
    train_feat = features_of(train_hidden, train_cotangent, proj_hidden, proj_cotangent, train_lengths).astype(jnp.float32)
    test_feat = features_of(test_hidden, test_cotangent, proj_hidden, proj_cotangent, test_lengths).astype(jnp.float32)
    count = train_feat.shape[0]
    raw = jnp.dot(train_feat.T, train_feat, precision=lax.Precision.HIGHEST)
    damping = 0.1 * jnp.trace(raw) / (count * K)
    gram = raw / count + damping * jnp.eye(K, dtype=jnp.float32)
    factor = jnp.linalg.cholesky(gram)
    solved = jax.scipy.linalg.cho_solve((factor, True), train_feat.T)
    weighted = solved.T.astype(jnp.bfloat16).astype(jnp.float32)
    return jnp.dot(weighted, test_feat.T, precision=lax.Precision.HIGHEST) * (1.0 / math.sqrt(K))
```

```python
import math

import jax
import jax.numpy as jnp
import numpy as np
from jax import lax
from jax.experimental import pallas as pl
from jax.experimental.pallas import tpu as pltpu
from jax.sharding import PartitionSpec as P

KX = 32
KG = 64
K = 2048
TOKS = 8
COUNT = 8192
GROUP = 256
GROUPS = K // GROUP
EXTRA = 136
TOL = 2.0**-12
MAX_STEPS = 8192

TASKS = [(i, j) for i in range(GROUPS) for j in range(i + 1, GROUPS)]
N_OFF = len(TASKS)
TASKS = TASKS + [(2 * k, 2 * k + 1) for k in range(GROUPS // 2)]

F32 = jnp.float32
BF16 = jnp.bfloat16
CORE_SWAP = [(0, 1), (1, 0), (2, 3), (3, 2)]
FAR_SWAP = [(0, 2), (2, 0), (1, 3), (3, 1)]
SAME_CORE = [[d * 4 + h * 2 + c for d in range(32) for h in range(2)] for c in range(2)]


def vmem_spec():
    return pl.BlockSpec(memory_space=pltpu.VMEM)


def params(mib):
    return pltpu.CompilerParams(vmem_limit_bytes=mib * 1024 * 1024)


def project_kernel(h_ref, ht_ref, c_ref, ct_ref, ph_ref, pc_ref, out_ref, right, right_te):
    t = pl.program_id(0)
    left = jnp.dot(ph_ref[...], h_ref[0], preferred_element_type=F32)
    left_te = jnp.dot(ph_ref[...], ht_ref[0], preferred_element_type=F32)
    blank = jnp.zeros((KX, 32), F32)
    for q in range(4):
        out_ref[q, t, 0:KX, :] = jnp.concatenate(
            [left[:, 64 * q : 64 * q + 64], left_te[:, 32 * q : 32 * q + 32], blank], axis=1
        )
    nt = (((1,), (1,)), ((), ()))
    right[pl.ds(pl.multiple_of(t * 256, 256), 256), 0:KG] = lax.dot_general(
        c_ref[...], pc_ref[...], nt, preferred_element_type=F32
    )
    right_te[pl.ds(pl.multiple_of(t * 128, 128), 128), 0:KG] = lax.dot_general(
        ct_ref[...], pc_ref[...], nt, preferred_element_type=F32
    )

    @pl.when(t == TOKS - 1)
    def _():
        pad = jnp.zeros((KG, 32), F32)
        for s in range(TOKS):
            b = right[pl.ds(s, 256, stride=TOKS), :].T[0:KG]
            bt = right_te[pl.ds(s, 128, stride=TOKS), :].T[0:KG]
            for q in range(4):
                out_ref[q, s, KX : KX + KG, :] = jnp.concatenate(
                    [b[:, 64 * q : 64 * q + 64], bt[:, 32 * q : 32 * q + 32], pad], axis=1
                )


def project(hidden, hidden_te, cot, cot_te, ph, pc):
    ff = hidden.shape[1]
    d = cot.shape[1]
    return pl.pallas_call(
        project_kernel,
        grid=(TOKS,),
        in_specs=[
            pl.BlockSpec((1, ff, 256), lambda t: (t, 0, 0)),
            pl.BlockSpec((1, ff, 128), lambda t: (t, 0, 0)),
            pl.BlockSpec((256, d), lambda t: (t, 0)),
            pl.BlockSpec((128, d), lambda t: (t, 0)),
            pl.BlockSpec((KX, ff), lambda t: (0, 0)),
            pl.BlockSpec((KG, d), lambda t: (0, 0)),
        ],
        out_specs=pl.BlockSpec((4, TOKS, KX + KG, 128), lambda t: (0, 0, 0, 0)),
        out_shape=jax.ShapeDtypeStruct((4, TOKS, KX + KG, 128), F32),
        scratch_shapes=[pltpu.VMEM((2048, 128), F32), pltpu.VMEM((1024, 128), F32)],
        compiler_params=params(40),
        name="project",
    )(hidden, hidden_te, cot, cot_te, ph, pc)


def feature_kernel(mine_ref, got_ref, lens_ref, send_ref, train_ref, test_ref, right, feat):
    lens = lens_ref[...]
    left = []
    for t in range(TOKS):
        left.append(jnp.where(lens > t, mine_ref[t, 0:KX, :] + got_ref[t, 0:KX, :], 0.0))
        right[t] = mine_ref[t, KX : KX + KG, :] + got_ref[t, KX : KX + KG, :]
    for j in range(KG):
        acc = left[0] * right[0, j : j + 1, :]
        for t in range(1, TOKS):
            acc += left[t] * right[t, j : j + 1, :]
        feat[j * KX : (j + 1) * KX, :] = acc
    for k in range(K // 128):
        block = feat[k * 128 : (k + 1) * 128, :].T.astype(BF16)
        lanes = slice(k * 128, (k + 1) * 128)
        train_ref[:, lanes] = block[0:64]
        test_ref[:, lanes] = block[64:96]
        group, part = divmod(k * 128, GROUP)
        for n, (i, j) in enumerate(TASKS):
            if i == group:
                send_ref[n, :, part : part + 128] = block[0:64]
            if j == group:
                send_ref[n, :, GROUP + part : GROUP + part + 128] = block[0:64]


def features(mine, got, lens):
    return pl.pallas_call(
        feature_kernel,
        in_specs=[vmem_spec()] * 3,
        out_specs=[vmem_spec()] * 3,
        out_shape=[
            jax.ShapeDtypeStruct((32, 64, 2 * GROUP), BF16),
            jax.ShapeDtypeStruct((64, K), BF16),
            jax.ShapeDtypeStruct((32, K), BF16),
        ],
        scratch_shapes=[pltpu.VMEM((TOKS, KG, 128), F32), pltpu.VMEM((K, 128), F32)],
        compiler_params=params(40),
        name="features",
    )(mine, got, lens)


def gram_kernel(pair_ref, rows_ref, out_ref, block):
    left = rows_ref[:, 0:GROUP]
    right = rows_ref[:, GROUP : 2 * GROUP]
    tn = (((0,), (0,)), ((), ()))
    out_ref[:, 128:EXTRA, :] = jnp.zeros((4, EXTRA - 128, 128), F32)

    @pl.when(pair_ref[0] == 0)
    def _():
        block[...] = lax.dot_general(left, right, tn, preferred_element_type=F32)

    @pl.when(pair_ref[0] == 1)
    def _():
        low = lax.dot_general(left, left, tn, preferred_element_type=F32)
        high = lax.dot_general(right, right, tn, preferred_element_type=F32)
        row = lax.broadcasted_iota(jnp.int32, (GROUP, GROUP), 0)
        col = lax.broadcasted_iota(jnp.int32, (GROUP, GROUP), 1)
        block[...] = jnp.where(row >= col, low, high)
        diag = jnp.sum(jnp.where(row == col, high, 0.0), axis=0, keepdims=True)
        for q in range(4):
            out_ref[q, 128:129, :] = diag[:, 0:128]
            out_ref[q, 129:130, :] = diag[:, 128:256]

    for q in range(4):
        out_ref[q, 0:64, :] = block[64 * q : 64 * q + 64, 0:128]
        out_ref[q, 64:128, :] = block[64 * q : 64 * q + 64, 128:256]


def gram_block(pair, rows):
    return pl.pallas_call(
        gram_kernel,
        in_specs=[pl.BlockSpec(memory_space=pltpu.SMEM), vmem_spec()],
        out_specs=vmem_spec(),
        out_shape=jax.ShapeDtypeStruct((4, EXTRA, 128), F32),
        scratch_shapes=[pltpu.VMEM((GROUP, GROUP), F32)],
        compiler_params=params(40),
        name="gram_block",
    )(pair, rows)


def split_kernel(mine_ref, got_ref, high_ref, low_ref):
    total = mine_ref[...] + got_ref[...]
    high = total.astype(BF16)
    low = (total - high.astype(F32)).astype(BF16)
    for n in range(64):
        high_ref[n] = high
        low_ref[n] = low


def split(mine, got):
    shape = jax.ShapeDtypeStruct((64, EXTRA, 128), BF16)
    return pl.pallas_call(
        split_kernel,
        in_specs=[vmem_spec()] * 2,
        out_specs=[vmem_spec()] * 2,
        out_shape=[shape, shape],
        compiler_params=params(40),
        name="split",
    )(mine, got)


def unpack(parts, out):
    row = lax.broadcasted_iota(jnp.int32, (GROUP, GROUP), 0)
    col = lax.broadcasted_iota(jnp.int32, (GROUP, GROUP), 1)
    trace = jnp.zeros((1, GROUP), F32)
    for n, (i, j) in enumerate(TASKS):
        pieces = []
        for q in range(4):
            h, c = divmod(q, 2)
            pieces.append(
                jnp.concatenate(
                    [parts[c, 2 * n + h, 0:64, :], parts[c, 2 * n + h, 64:128, :]], axis=1
                )
            )
        block = jnp.concatenate(pieces, axis=0)
        i0, j0 = i * GROUP, j * GROUP
        if n < N_OFF:
            out[i0 : i0 + GROUP, j0 : j0 + GROUP] = block
            out[j0 : j0 + GROUP, i0 : i0 + GROUP] = block.T
        else:
            wide = block.astype(F32)
            flipped = wide.T
            tail = parts[0, 2 * n, 128:EXTRA, :].astype(F32)
            diag = jnp.concatenate([tail[0:1], tail[1:2]], axis=1)
            low = jnp.where(row >= col, wide, flipped)
            high = jnp.where(row < col, wide, jnp.where(row > col, flipped, diag))
            trace += jnp.sum(jnp.where(row == col, wide, 0.0), axis=0, keepdims=True) + diag
            out[i0 : i0 + GROUP, i0 : i0 + GROUP] = low.astype(BF16)
            out[j0 : j0 + GROUP, j0 : j0 + GROUP] = high.astype(BF16)
    return jnp.sum(trace, axis=1, keepdims=True)


def rows_dot(a, b):
    return jnp.sum(a * b, axis=1, keepdims=True)


def solve_kernel(
    core_ref,
    high_own,
    high_other,
    low_own,
    low_other,
    f_ref,
    w_ref,
    parts_high,
    parts_low,
    high,
    low,
    x,
    r,
    p,
    y,
    sems,
):
    core = core_ref[0]
    copies = [
        pltpu.make_async_copy(high_own, parts_high.at[core], sems.at[0]),
        pltpu.make_async_copy(high_other, parts_high.at[1 - core], sems.at[1]),
        pltpu.make_async_copy(low_own, parts_low.at[core], sems.at[2]),
        pltpu.make_async_copy(low_other, parts_low.at[1 - core], sems.at[3]),
    ]
    for copy in copies:
        copy.start()
    f = f_ref[...].astype(F32)
    top = jnp.max(jnp.abs(f), axis=1, keepdims=True)
    top = jnp.where(top > 0.0, top, 1.0)
    f = f / top
    r[...] = f
    p[...] = f
    x[...] = jnp.zeros_like(f)
    copies[0].wait()
    copies[1].wait()
    trace = unpack(parts_high, high)
    copies[2].wait()
    copies[3].wait()
    trace = trace + unpack(parts_low, low)
    gain = K / trace

    def matvec():
        whole = p[...]
        upper = whole.astype(BF16)
        lower = (whole - upper.astype(F32)).astype(BF16)
        both = jnp.concatenate([upper, lower], axis=0)
        for n in range(GROUPS):
            cols = slice(n * GROUP, (n + 1) * GROUP)
            main = jnp.dot(both, high[:, cols], preferred_element_type=F32)
            rest = jnp.dot(upper, low[:, cols], preferred_element_type=F32)
            y[:, cols] = (main[0:64] + main[64:128] + rest) * gain + 0.1 * whole[:, cols]

    def more(state):
        step, rr, left = state
        return jnp.logical_and(step < MAX_STEPS, left > 0.0)

    def advance(state):
        step, rr, _ = state
        matvec()
        py = rows_dot(p[...], y[...])
        alpha = rr / jnp.where(py > 0.0, py, 1.0)
        x[...] += alpha * p[...]
        r[...] -= alpha * y[...]
        new = rows_dot(r[...], r[...])
        xx = rows_dot(x[...], x[...])
        beta = new / jnp.where(rr > 0.0, rr, 1.0)
        p[...] = r[...] + beta * p[...]
        left = jnp.max(new - (0.1 * TOL) ** 2 * xx)
        return step + 1, new, left

    rr = rows_dot(f, f)
    lax.while_loop(more, advance, (jnp.int32(0), rr, jnp.max(rr)))
    w_ref[...] = (x[...] * (top * (COUNT * K / trace))).astype(BF16)


def solve(core, high_own, high_other, low_own, low_other, f):
    any_spec = pl.BlockSpec(memory_space=pl.ANY)
    return pl.pallas_call(
        solve_kernel,
        in_specs=[pl.BlockSpec(memory_space=pltpu.SMEM)] + [any_spec] * 4 + [vmem_spec()],
        out_specs=vmem_spec(),
        out_shape=jax.ShapeDtypeStruct((64, K), BF16),
        scratch_shapes=[
            pltpu.VMEM((2, 64, EXTRA, 128), BF16),
            pltpu.VMEM((2, 64, EXTRA, 128), BF16),
            pltpu.VMEM((K, K), BF16),
            pltpu.VMEM((K, K), BF16),
            pltpu.VMEM((64, K), F32),
            pltpu.VMEM((64, K), F32),
            pltpu.VMEM((64, K), F32),
            pltpu.VMEM((64, K), F32),
            pltpu.SemaphoreType.DMA((4,)),
        ],
        cost_estimate=pl.CostEstimate(flops=6 * 10**10, bytes_accessed=2 * 10**7, transcendentals=0),
        compiler_params=params(56),
        name="solve",
    )(core, high_own, high_other, low_own, low_other, f)


def place_kernel(place_ref, *refs):
    out_ref = refs[-1]
    for me in range(4):

        @pl.when(place_ref[0] == me)
        def _():
            for d in range(32):
                span = slice(32 * d, 32 * d + 32)
                out_ref[:, 128 * d : 128 * d + 128] = jnp.concatenate(
                    [refs[me ^ q][:, span].astype(F32) for q in range(4)], axis=1
                )


def place(index, parts):
    return pl.pallas_call(
        place_kernel,
        in_specs=[pl.BlockSpec(memory_space=pltpu.SMEM)] + [vmem_spec()] * 4,
        out_specs=vmem_spec(),
        out_shape=jax.ShapeDtypeStruct((64, 4096), F32),
        compiler_params=params(40),
        name="place",
    )(index, *parts)


def scatter_sum(parts, far, core):
    pairs = parts.reshape((2, 2) + parts.shape[1:])
    other = lax.dynamic_index_in_dim(pairs, 1 - core, 1, keepdims=False)
    keep = lax.dynamic_index_in_dim(pairs, core, 1, keepdims=False)
    both = keep + lax.ppermute(other, "proj", CORE_SWAP)
    got = lax.ppermute(
        lax.dynamic_index_in_dim(both, 1 - far, 0, keepdims=False), "proj", FAR_SWAP
    )
    return lax.dynamic_index_in_dim(both, far, 0, keepdims=False), got


def share(chunks):
    own = lax.all_to_all(
        chunks, ("dp", "proj"), 0, 0, axis_index_groups=SAME_CORE, tiled=True
    )
    return own, lax.ppermute(own, "proj", CORE_SWAP)


def per_device(
    train_hidden,
    train_cotangent,
    test_hidden,
    test_cotangent,
    proj_hidden,
    proj_cotangent,
    train_lengths,
    test_lengths,
):
    quarter = lax.axis_index("proj")
    far, core = quarter // 2, quarter % 2
    task = lax.axis_index("dp")
    d = train_cotangent.shape[2]
    partial_sums = project(
        jnp.transpose(train_hidden, (1, 2, 0)),
        jnp.transpose(test_hidden, (1, 2, 0)),
        train_cotangent.reshape(-1, d),
        test_cotangent.reshape(-1, d),
        proj_hidden.T,
        proj_cotangent.T,
    )
    lens = jnp.concatenate(
        [
            lax.dynamic_slice_in_dim(train_lengths, quarter * 64, 64),
            lax.dynamic_slice_in_dim(test_lengths, quarter * 32, 32),
            jnp.zeros((32,), jnp.int32),
        ]
    )[None]
    mine, got = scatter_sum(partial_sums, far, core)
    send, train, test = features(mine, got, lens)
    tests = lax.all_gather(test, "dp", axis=0, tiled=True)
    rows = lax.all_to_all(send, "dp", 0, 0, tiled=True).reshape(2048, 2 * GROUP)
    pair = (task >= N_OFF).astype(jnp.int32).reshape(1)
    mine, got = scatter_sum(gram_block(pair, rows), far, core)
    high, low = split(mine, got)
    high_own, high_other = share(high)
    low_own, low_other = share(low)
    weighted = solve(core.reshape(1), high_own, high_other, low_own, low_other, train)
    near = jnp.concatenate([weighted, lax.ppermute(weighted, "proj", FAR_SWAP)], axis=0)
    others = lax.ppermute(near, "proj", CORE_SWAP)
    nt = (((1,), (1,)), ((), ()))
    scale = 1.0 / math.sqrt(K)
    a = lax.dot_general(near, tests, nt, preferred_element_type=F32) * scale
    b = lax.dot_general(others, tests, nt, preferred_element_type=F32) * scale
    got_b = lax.ppermute(b, "proj", CORE_SWAP)
    crossing = jnp.concatenate([a[64:128], got_b[64:128]], axis=0)
    got_c = lax.ppermute(crossing, "proj", FAR_SWAP)
    return place(quarter.reshape(1), [a[0:64], got_b[0:64], got_c[0:64], got_c[64:128]])


def solution(mesh):
    in_specs = (
        P("dp", None, "proj"),
        P("dp", None, "proj"),
        P("dp", None, "proj"),
        P("dp", None, "proj"),
        P("proj", None),
        P("proj", None),
        P("dp"),
        P("dp"),
    )
    out_specs = P(("dp", "proj"), None)
    return jax.shard_map(
        per_device, mesh=mesh, in_specs=in_specs, out_specs=out_specs, check_vma=False
    )
```

```python
import functools
import math

import jax
import jax.numpy as jnp
import numpy as np
from jax import lax
from jax.experimental import pallas as pl
from jax.experimental.pallas import tpu as pltpu
from jax.sharding import PartitionSpec as P

KX = 32
KG = 64
K = 2048
TOKS = 8
COUNT = 8192
GROUP = 256
GROUPS = K // GROUP
EXTRA = 136
TOL = 2.0**-9
START_STEPS = 13
START_FLOPS = 10**9
FINISH_FLOPS = 10**9
MAX_STEPS = 8192

TASKS = [(i, j) for i in range(GROUPS) for j in range(i + 1, GROUPS)]
N_OFF = len(TASKS)
TASKS = TASKS + [(2 * k, 2 * k + 1) for k in range(GROUPS // 2)]

F32 = jnp.float32
BF16 = jnp.bfloat16
CORE_SWAP = [(0, 1), (1, 0), (2, 3), (3, 2)]
FAR_SWAP = [(0, 2), (2, 0), (1, 3), (3, 1)]
NEAR = [[i, i + 16] for i in range(16)]
PLANES = [[h * 16 + i for i in range(16)] for h in range(2)]
SAME_CORE = [[d * 4 + h * 2 + c for d in range(32) for h in range(2)] for c in range(2)]


def vmem_spec():
    return pl.BlockSpec(memory_space=pltpu.VMEM)


def params(mib):
    return pltpu.CompilerParams(vmem_limit_bytes=mib * 1024 * 1024)


def project_kernel(
    at_ref,
    h_ref,
    ht_ref,
    c_ref,
    ct_ref,
    ph_ref,
    pc_ref,
    send_ref,
    keep_ref,
    h,
    ht,
    c,
    ct,
    ph,
    pc,
    left,
    left_te,
    right,
    right_te,
    chunks,
    sems,
):
    def token(t):
        return (
            pltpu.make_async_copy(h_ref.at[t], h.at[t], sems.at[4 + t]),
            pltpu.make_async_copy(ht_ref.at[t], ht.at[t], sems.at[4 + TOKS + t]),
        )

    first = [
        pltpu.make_async_copy(src, dst, sems.at[n])
        for n, (src, dst) in enumerate([(pc_ref, pc), (c_ref, c), (ct_ref, ct), (ph_ref, ph)])
    ]
    for copy in first:
        copy.start()
    for t in range(TOKS):
        for copy in token(t):
            copy.start()

    nt = (((1,), (1,)), ((), ()))
    first[0].wait()
    for n, src, dst, slots, base in ((1, c, right, 4, 0), (2, ct, right_te, 2, 4)):
        first[n].wait()
        dst[:, 0:KG] = lax.dot_general(src[...], pc[...], nt, preferred_element_type=F32)
        examples = dst.shape[0] // TOKS
        parts = TOKS // slots
        width = examples // 4
        for u in range(slots):
            tall = [dst[pl.ds(p * slots + u, examples, stride=TOKS), :].T for p in range(parts)]
            for q in range(4):
                chunks[q, base + u, KX : KX + KG, :] = jnp.concatenate(
                    [piece[0:KG, width * q : width * (q + 1)] for piece in tall], axis=1
                )
    first[3].wait()

    def step(t, carry):
        for copy in token(t):
            copy.wait()
        left[t] = jnp.dot(ph[...], h[t], preferred_element_type=F32)
        left_te[t] = jnp.dot(ph[...], ht[t], preferred_element_type=F32)
        return carry

    lax.fori_loop(0, TOKS, step, 0)
    for src, slots, base in ((left, 4, 0), (left_te, 2, 4)):
        parts = TOKS // slots
        width = src.shape[2] // 4
        for u in range(slots):
            for q in range(4):
                chunks[q, base + u, 0:KX, :] = jnp.concatenate(
                    [src[p * slots + u, :, width * q : width * (q + 1)] for p in range(parts)],
                    axis=1,
                )
    for q in range(4):
        side, core = divmod(q, 2)
        slot = jnp.where(at_ref[1] == side, 0, 1)

        @pl.when(at_ref[0] == core)
        def _():
            keep_ref[slot] = chunks[q]

        @pl.when(at_ref[0] != core)
        def _():
            send_ref[slot] = chunks[q]


def project(at, hidden, hidden_te, cot, cot_te, ph, pc):
    shape = jax.ShapeDtypeStruct((2, 6, KX + KG, 128), F32)
    arrays = [hidden, hidden_te, cot, cot_te, ph, pc]
    any_spec = pl.BlockSpec(memory_space=pl.ANY)
    return pl.pallas_call(
        project_kernel,
        in_specs=[pl.BlockSpec(memory_space=pltpu.SMEM)] + [any_spec] * 6,
        out_specs=[vmem_spec()] * 2,
        out_shape=[shape, shape],
        scratch_shapes=[pltpu.VMEM(array.shape, BF16) for array in arrays]
        + [
            pltpu.VMEM((TOKS, KX, 256), F32),
            pltpu.VMEM((TOKS, KX, 128), F32),
            pltpu.VMEM((2048, 128), F32),
            pltpu.VMEM((1024, 128), F32),
            pltpu.VMEM((4, 6, KX + KG, 128), F32),
            pltpu.SemaphoreType.DMA((4 + 2 * TOKS,)),
        ],
        compiler_params=params(60),
        cost_estimate=pl.CostEstimate(flops=10**9, bytes_accessed=3 * 10**7, transcendentals=0),
        name="project",
    )(at, *arrays)


def feature_kernel(mine_ref, got_ref, lens_ref, train_ref, test_ref, send_ref, right, feat):
    for base, slots, out_ref in ((0, 4, train_ref), (4, 2, test_ref)):
        parts = TOKS // slots
        width = 128 // parts
        lens = lens_ref[base // 4 : base // 4 + 1, :]
        part = lax.broadcasted_iota(jnp.int32, (1, 128), 1) // width
        left = []
        for u in range(slots):
            at = base + u
            valid = lens > part * slots + u
            left.append(jnp.where(valid, mine_ref[at, 0:KX, :] + got_ref[at, 0:KX, :], 0.0))
            right[u] = mine_ref[at, KX : KX + KG, :] + got_ref[at, KX : KX + KG, :]
        for j in range(KG):
            acc = left[0] * right[0, j : j + 1, :]
            for u in range(1, slots):
                acc += left[u] * right[u, j : j + 1, :]
            feat[j * KX : (j + 1) * KX, :] = acc
        for k in range(K // 128):
            tall = feat[k * 128 : (k + 1) * 128, :].T
            block = tall[0:width]
            for p in range(1, parts):
                block += tall[p * width : (p + 1) * width]
            block = block.astype(BF16)
            out_ref[:, k * 128 : (k + 1) * 128] = block
            if base:
                continue
            group, off = divmod(k * 128, GROUP)
            for n, (i, j) in enumerate(TASKS):
                if i == group:
                    send_ref[n, :, off : off + 128] = block
                if j == group:
                    send_ref[n, :, GROUP + off : GROUP + off + 128] = block


def features(mine, got, lens):
    return pl.pallas_call(
        feature_kernel,
        in_specs=[vmem_spec()] * 3,
        out_specs=[vmem_spec()] * 3,
        out_shape=[
            jax.ShapeDtypeStruct((64, K), BF16),
            jax.ShapeDtypeStruct((32, K), BF16),
            jax.ShapeDtypeStruct((32, 64, 2 * GROUP), BF16),
        ],
        scratch_shapes=[pltpu.VMEM((4, KG, 128), F32), pltpu.VMEM((K, 128), F32)],
        compiler_params=params(40),
        name="features",
    )(mine, got, lens)


def gram_kernel(at_ref, rows_ref, send_ref, keep_ref, block, tail):
    left = rows_ref[:, 0:GROUP]
    right = rows_ref[:, GROUP : 2 * GROUP]
    tn = (((0,), (0,)), ((), ()))
    tail[...] = jnp.zeros((EXTRA - 128, 128), F32)

    @pl.when(at_ref[2] == 0)
    def _():
        block[...] = lax.dot_general(left, right, tn, preferred_element_type=F32)

    @pl.when(at_ref[2] == 1)
    def _():
        low = lax.dot_general(left, left, tn, preferred_element_type=F32)
        high = lax.dot_general(right, right, tn, preferred_element_type=F32)
        row = lax.broadcasted_iota(jnp.int32, (GROUP, GROUP), 0)
        col = lax.broadcasted_iota(jnp.int32, (GROUP, GROUP), 1)
        block[...] = jnp.where(row >= col, low, high)
        diag = jnp.sum(jnp.where(row == col, high, 0.0), axis=0, keepdims=True)
        tail[0:1, :] = diag[:, 0:128]
        tail[1:2, :] = diag[:, 128:256]

    def fill(ref, slot, q):
        ref[slot, 0:64, :] = block[64 * q : 64 * q + 64, 0:128]
        ref[slot, 64:128, :] = block[64 * q : 64 * q + 64, 128:256]
        ref[slot, 128:EXTRA, :] = tail[...]

    for q in range(4):
        side, core = divmod(q, 2)
        slot = jnp.where(at_ref[1] == side, 0, 1)

        @pl.when(at_ref[0] == core)
        def _():
            fill(keep_ref, slot, q)

        @pl.when(at_ref[0] != core)
        def _():
            fill(send_ref, slot, q)


def gram_block(at, rows):
    shape = jax.ShapeDtypeStruct((2, EXTRA, 128), F32)
    return pl.pallas_call(
        gram_kernel,
        in_specs=[pl.BlockSpec(memory_space=pltpu.SMEM), vmem_spec()],
        out_specs=[vmem_spec()] * 2,
        out_shape=[shape, shape],
        scratch_shapes=[pltpu.VMEM((GROUP, GROUP), F32), pltpu.VMEM((EXTRA - 128, 128), F32)],
        compiler_params=params(40),
        name="gram_block",
    )(at, rows)


def split_kernel(want_low, mine_ref, got_ref, out_ref):
    total = mine_ref[...] + got_ref[...]
    part = total.astype(BF16)
    if want_low:
        part = (total - part.astype(F32)).astype(BF16)
    for n in range(64):
        out_ref[n] = part


def split(mine, got, want_low):
    return pl.pallas_call(
        functools.partial(split_kernel, want_low),
        in_specs=[vmem_spec()] * 2,
        out_specs=vmem_spec(),
        out_shape=jax.ShapeDtypeStruct((64, EXTRA, 128), BF16),
        compiler_params=params(60),
        name="split_low" if want_low else "split_high",
    )(mine, got)


def unpack(core, own, other, out, trace_ref):
    @pl.when(core == 0)
    def _():
        unpack_parts((own, other), out, trace_ref)

    @pl.when(core == 1)
    def _():
        unpack_parts((other, own), out, trace_ref)

    return jnp.sum(trace_ref[0:1, :], axis=1, keepdims=True)


def unpack_parts(parts, out, trace_ref):
    row = lax.broadcasted_iota(jnp.int32, (GROUP, GROUP), 0)
    col = lax.broadcasted_iota(jnp.int32, (GROUP, GROUP), 1)
    trace = jnp.zeros((1, GROUP), F32)
    for n, (i, j) in enumerate(TASKS):
        pieces = []
        for q in range(4):
            h, c = divmod(q, 2)
            pieces.append(
                jnp.concatenate(
                    [parts[c][2 * n + h, 0:64, :], parts[c][2 * n + h, 64:128, :]], axis=1
                )
            )
        block = jnp.concatenate(pieces, axis=0)
        i0, j0 = i * GROUP, j * GROUP
        if n < N_OFF:
            out[i0 : i0 + GROUP, j0 : j0 + GROUP] = block
            out[j0 : j0 + GROUP, i0 : i0 + GROUP] = block.T
        else:
            wide = block.astype(F32)
            flipped = wide.T
            tail = parts[0][2 * n, 128:EXTRA, :].astype(F32)
            diag = jnp.concatenate([tail[0:1], tail[1:2]], axis=1)
            low = jnp.where(row >= col, wide, flipped)
            high = jnp.where(row < col, wide, jnp.where(row > col, flipped, diag))
            trace += jnp.sum(jnp.where(row == col, wide, 0.0), axis=0, keepdims=True) + diag
            out[i0 : i0 + GROUP, i0 : i0 + GROUP] = low.astype(BF16)
            out[j0 : j0 + GROUP, j0 : j0 + GROUP] = high.astype(BF16)
    trace_ref[0:1, :] = trace


def rows_dot(a, b):
    return jnp.sum(a * b, axis=1, keepdims=True)


BLOCKS = [slice(n * GROUP, (n + 1) * GROUP) for n in range(GROUPS)]


def product(high, low, p, y, gain):
    upper = [p[:, cols].astype(BF16) for cols in BLOCKS]
    left = jnp.concatenate(upper, axis=1)
    if low is not None:
        lower = [(p[:, cols] - up.astype(F32)).astype(BF16) for cols, up in zip(BLOCKS, upper)]
        both = jnp.concatenate([left, jnp.concatenate(lower, axis=1)], axis=0)
    total = jnp.zeros((64, GROUP), F32)
    for cols in BLOCKS:
        if low is None:
            main = jnp.dot(left, high[:, cols], preferred_element_type=F32)
        else:
            main = jnp.dot(both, high[:, cols], preferred_element_type=F32)
            rest = jnp.dot(left, low[:, cols], preferred_element_type=F32)
            main = main[0:64] + main[64:128] + rest
        value = main * gain + 0.1 * p[:, cols]
        y[:, cols] = value
        total += value * p[:, cols]
    return jnp.sum(total, axis=1, keepdims=True)


def advance(high, low, x, r, p, y, gain, rr):
    py = product(high, low, p, y, gain)
    alpha = jnp.where(py > 0.0, rr / jnp.where(py > 0.0, py, 1.0), 0.0)
    new = jnp.zeros((64, GROUP), F32)
    xx = jnp.zeros((64, GROUP), F32)
    for cols in BLOCKS:
        xv = x[:, cols] + alpha * p[:, cols]
        rv = r[:, cols] - alpha * y[:, cols]
        x[:, cols] = xv
        r[:, cols] = rv
        xx += xv * xv
        new += rv * rv
    new = jnp.sum(new, axis=1, keepdims=True)
    beta = new / jnp.where(rr > 0.0, rr, 1.0)
    for cols in BLOCKS:
        p[:, cols] = r[:, cols] + beta * p[:, cols]
    return new, jnp.sum(xx, axis=1, keepdims=True)


def scaled(f_ref):
    f = f_ref[...].astype(F32)
    top = jnp.max(jnp.abs(f), axis=1, keepdims=True)
    top = jnp.where(top > 0.0, top, 1.0)
    return f / top, top


def start_kernel(
    core_ref, own, other, f_ref, x0_ref, base_ref, trace_ref, gram, high, x, r, p, y, sem
):
    f, _ = scaled(f_ref)
    r[...] = f
    p[...] = f
    x[...] = jnp.zeros_like(f)
    gain = K / unpack(core_ref[0], own, other, high, trace_ref)
    keep = pltpu.make_async_copy(high, gram, sem)
    keep.start()
    lax.fori_loop(
        0,
        START_STEPS,
        lambda _, rr: advance(high, None, x, r, p, y, gain, rr)[0],
        rows_dot(f, f),
    )
    x0 = x[...].astype(BF16)
    x0_ref[...] = x0
    for cols in BLOCKS:
        base_ref[:, cols] = jnp.dot(x0, high[:, cols], preferred_element_type=F32)
    keep.wait()


def solve_start(core, own, other, f):
    return pl.pallas_call(
        start_kernel,
        in_specs=[pl.BlockSpec(memory_space=pltpu.SMEM)] + [vmem_spec()] * 3,
        out_specs=[vmem_spec()] * 3 + [pl.BlockSpec(memory_space=pl.ANY)],
        out_shape=[
            jax.ShapeDtypeStruct((64, K), BF16),
            jax.ShapeDtypeStruct((64, K), F32),
            jax.ShapeDtypeStruct((8, GROUP), F32),
            jax.ShapeDtypeStruct((K, K), BF16),
        ],
        scratch_shapes=[
            pltpu.VMEM((K, K), BF16),
            pltpu.VMEM((64, K), F32),
            pltpu.VMEM((64, K), F32),
            pltpu.VMEM((64, K), F32),
            pltpu.VMEM((64, K), F32),
            pltpu.SemaphoreType.DMA,
        ],
        cost_estimate=pl.CostEstimate(flops=START_FLOPS, bytes_accessed=10**7, transcendentals=0),
        compiler_params=params(60),
        name="solve_start",
    )(core, own, other, f)


def finish_kernel(
    core_ref,
    own,
    other,
    gram,
    f_ref,
    x0_ref,
    base_ref,
    trace_ref,
    w_ref,
    high,
    low,
    low_trace,
    x,
    r,
    p,
    y,
    sem,
):
    load = pltpu.make_async_copy(gram, high, sem)
    load.start()
    f, top = scaled(f_ref)
    trace = jnp.sum(trace_ref[0:1, :], axis=1, keepdims=True)
    trace = trace + unpack(core_ref[0], own, other, low, low_trace)
    gain = K / trace
    x0 = x0_ref[...]
    for cols in BLOCKS:
        main = base_ref[:, cols] + jnp.dot(x0, low[:, cols], preferred_element_type=F32)
        y[:, cols] = main * gain + 0.1 * x0_ref[:, cols].astype(F32)
    ff = rows_dot(f, f)
    rest = f - y[...]
    rr = rows_dot(rest, rest)
    good = rr <= ff
    rr = jnp.where(good, rr, ff)
    first = jnp.where(good, x0.astype(F32), 0.0)
    rest = jnp.where(good, rest, f)
    x[...] = first
    r[...] = rest
    p[...] = rest
    load.wait()

    def excess(rr, xx):
        return jnp.max(rr - (0.1 * TOL) ** 2 * xx)

    def more(state):
        return jnp.logical_and(state[0] < MAX_STEPS, state[2] > 0.0)

    def body(state):
        step, rr, _ = state
        rr, xx = advance(high, low, x, r, p, y, gain, rr)
        return step + 1, rr, excess(rr, xx)

    lax.while_loop(more, body, (jnp.int32(0), rr, excess(rr, rows_dot(first, first))))
    w_ref[...] = (x[...] * (top * (COUNT * K / trace))).astype(BF16)


def solve_finish(core, own, other, high, f, x0, base, trace):
    return pl.pallas_call(
        finish_kernel,
        in_specs=[pl.BlockSpec(memory_space=pltpu.SMEM)] + [vmem_spec()] * 2
        + [pl.BlockSpec(memory_space=pl.ANY)]
        + [vmem_spec()] * 4,
        out_specs=vmem_spec(),
        out_shape=jax.ShapeDtypeStruct((64, K), BF16),
        scratch_shapes=[
            pltpu.VMEM((K, K), BF16),
            pltpu.VMEM((K, K), BF16),
            pltpu.VMEM((8, GROUP), F32),
            pltpu.VMEM((64, K), F32),
            pltpu.VMEM((64, K), F32),
            pltpu.VMEM((64, K), F32),
            pltpu.VMEM((64, K), F32),
            pltpu.SemaphoreType.DMA,
        ],
        cost_estimate=pl.CostEstimate(flops=FINISH_FLOPS, bytes_accessed=10**7, transcendentals=0),
        compiler_params=params(46),
        name="solve_finish",
    )(core, own, other, high, f, x0, base, trace)


def place_kernel(place_ref, *refs):
    out_ref = refs[-1]
    for me in range(4):

        @pl.when(2 * place_ref[1] + place_ref[0] == me)
        def _():
            for d in range(32):
                at = 64 * (d % 16) + 32 * (d // 16)
                out_ref[:, 128 * d : 128 * d + 128] = jnp.concatenate(
                    [refs[me ^ q][:, at : at + 32].astype(F32) for q in range(4)], axis=1
                )


def place(index, parts):
    return pl.pallas_call(
        place_kernel,
        in_specs=[pl.BlockSpec(memory_space=pltpu.SMEM)] + [vmem_spec()] * 4,
        out_specs=vmem_spec(),
        out_shape=jax.ShapeDtypeStruct((64, 4096), F32),
        compiler_params=params(40),
        name="place",
    )(index, *parts)


def fold(send, keep):
    recv = lax.ppermute(send, "proj", CORE_SWAP)
    return keep[0] + recv[0], lax.ppermute(keep[1] + recv[1], "proj", FAR_SWAP)


def exchange(chunks):
    return lax.all_to_all(
        chunks, ("dp", "proj"), 0, 0, axis_index_groups=SAME_CORE, tiled=True
    )


def per_device(
    train_hidden,
    train_cotangent,
    test_hidden,
    test_cotangent,
    proj_hidden,
    proj_cotangent,
    train_lengths,
    test_lengths,
):
    quarter = lax.axis_index("proj").astype(jnp.uint32)
    far, core = (quarter >> 1).astype(jnp.int32), (quarter & 1).astype(jnp.int32)
    task = lax.axis_index("dp")
    d = train_cotangent.shape[2]
    at = jnp.stack([core, far, (task >= N_OFF).astype(jnp.int32), core * 0])
    ph, pc = proj_hidden.T, proj_cotangent.T
    send, keep = project(
        at,
        jnp.transpose(train_hidden, (1, 2, 0)),
        jnp.transpose(test_hidden, (1, 2, 0)),
        train_cotangent.reshape(-1, d),
        test_cotangent.reshape(-1, d),
        ph,
        pc,
    )
    lens = jnp.stack(
        [
            jnp.tile(lax.dynamic_slice_in_dim(train_lengths, quarter * 64, 64), 2),
            jnp.tile(lax.dynamic_slice_in_dim(test_lengths, quarter * 32, 32), 4),
        ]
    )
    train, test, send = features(*fold(send, keep), lens)
    pairs = lax.all_gather(test, "dp", axis_index_groups=NEAR, axis=0, tiled=True)
    rows = lax.all_to_all(send, "dp", 0, 0, tiled=True).reshape(2048, 2 * GROUP)
    rows, pairs = lax.optimization_barrier((rows, pairs))
    tests = lax.all_gather(pairs, "dp", axis_index_groups=PLANES, axis=0, tiled=True)
    mine, got = fold(*gram_block(at, rows))
    high, low = split(mine, got, False), split(mine, got, True)
    high_own, low = lax.optimization_barrier((exchange(high), low))
    high_other = lax.ppermute(high_own, "proj", CORE_SWAP)
    low_own = exchange(low)
    x0, base, trace, gram = solve_start(at, high_own, high_other, train)
    low_own, x0 = lax.optimization_barrier((low_own, x0))
    low_other = lax.ppermute(low_own, "proj", CORE_SWAP)
    weighted = solve_finish(at, low_own, low_other, gram, train, x0, base, trace)
    weighted, tests = lax.optimization_barrier((weighted, tests))
    beyond = lax.ppermute(weighted, "proj", FAR_SWAP)
    tests_other = lax.ppermute(tests, "proj", CORE_SWAP)
    scale = 1.0 / math.sqrt(K)

    def scores(w, t):
        nt = (((1,), (1,)), ((), ()))
        return lax.dot_general(w, t, nt, preferred_element_type=F32) * scale

    near = scores(weighted, tests)
    beyond, near = lax.optimization_barrier((beyond, near))
    sent = jnp.concatenate([scores(beyond, tests), scores(beyond, tests_other)], axis=1)
    got = lax.ppermute(sent.astype(BF16), "proj", FAR_SWAP)
    return place(
        at,
        [near, scores(weighted, tests_other), got[:, 0:1024], got[:, 1024:]],
    )


def solution(mesh):
    in_specs = (
        P("dp", None, "proj"),
        P("dp", None, "proj"),
        P("dp", None, "proj"),
        P("dp", None, "proj"),
        P("proj", None),
        P("proj", None),
        P("dp"),
        P("dp"),
    )
    out_specs = P(("dp", "proj"), None)
    return jax.shard_map(
        per_device, mesh=mesh, in_specs=in_specs, out_specs=out_specs, check_vma=False
    )
```

```python
import functools
import math

import jax
import jax.numpy as jnp
import numpy as np
from jax import lax
from jax.experimental import pallas as pl
from jax.experimental.pallas import tpu as pltpu
from jax.sharding import PartitionSpec as P

KX = 32
KG = 64
K = 2048
TOKS = 8
COUNT = 8192
GROUP = 256
GROUPS = K // GROUP
EXTRA = 136
TOL = 2.0**-9
START_STEPS = 12
SLABS = 8
START_FLOPS = 10**9
FINISH_FLOPS = 10**9
MAX_STEPS = 8192

TASKS = [(i, j) for i in range(GROUPS) for j in range(i + 1, GROUPS)]
N_OFF = len(TASKS)
TASKS = TASKS + [(2 * k, 2 * k + 1) for k in range(GROUPS // 2)]

F32 = jnp.float32
BF16 = jnp.bfloat16
CORE_SWAP = [(0, 1), (1, 0), (2, 3), (3, 2)]
FAR_SWAP = [(0, 2), (2, 0), (1, 3), (3, 1)]
NEAR = [[i, i + 16] for i in range(16)]
PLANES = [[h * 16 + i for i in range(16)] for h in range(2)]
SAME_CORE = [[d * 4 + h * 2 + c for d in range(32) for h in range(2)] for c in range(2)]


def vmem_spec():
    return pl.BlockSpec(memory_space=pltpu.VMEM)


def params(mib):
    return pltpu.CompilerParams(vmem_limit_bytes=mib * 1024 * 1024)


def project_kernel(
    at_ref,
    h_ref,
    ht_ref,
    c_ref,
    ct_ref,
    ph_ref,
    pc_ref,
    send_ref,
    keep_ref,
    h,
    ht,
    c,
    ct,
    ph,
    pc,
    left,
    left_te,
    right,
    right_te,
    chunks,
    sems,
):
    def token(t):
        return (
            pltpu.make_async_copy(h_ref.at[t], h.at[t], sems.at[4 + t]),
            pltpu.make_async_copy(ht_ref.at[t], ht.at[t], sems.at[4 + TOKS + t]),
        )

    first = [
        pltpu.make_async_copy(src, dst, sems.at[n])
        for n, (src, dst) in enumerate([(pc_ref, pc), (c_ref, c), (ct_ref, ct), (ph_ref, ph)])
    ]
    for copy in first:
        copy.start()
    for t in range(TOKS):
        for copy in token(t):
            copy.start()

    nt = (((1,), (1,)), ((), ()))
    first[0].wait()
    for n, src, dst, slots, base in ((1, c, right, 4, 0), (2, ct, right_te, 2, 4)):
        first[n].wait()
        dst[:, 0:KG] = lax.dot_general(src[...], pc[...], nt, preferred_element_type=F32)
        examples = dst.shape[0] // TOKS
        parts = TOKS // slots
        width = examples // 4
        for u in range(slots):
            tall = [dst[pl.ds(p * slots + u, examples, stride=TOKS), :].T for p in range(parts)]
            for q in range(4):
                chunks[q, base + u, KX : KX + KG, :] = jnp.concatenate(
                    [piece[0:KG, width * q : width * (q + 1)] for piece in tall], axis=1
                )
    first[3].wait()

    def step(t, carry):
        for copy in token(t):
            copy.wait()
        left[t] = jnp.dot(ph[...], h[t], preferred_element_type=F32)
        left_te[t] = jnp.dot(ph[...], ht[t], preferred_element_type=F32)
        return carry

    lax.fori_loop(0, TOKS, step, 0)
    for src, slots, base in ((left, 4, 0), (left_te, 2, 4)):
        parts = TOKS // slots
        width = src.shape[2] // 4
        for u in range(slots):
            for q in range(4):
                chunks[q, base + u, 0:KX, :] = jnp.concatenate(
                    [src[p * slots + u, :, width * q : width * (q + 1)] for p in range(parts)],
                    axis=1,
                )
    for q in range(4):
        side, core = divmod(q, 2)
        slot = jnp.where(at_ref[1] == side, 0, 1)

        @pl.when(at_ref[0] == core)
        def _():
            keep_ref[slot] = chunks[q]

        @pl.when(at_ref[0] != core)
        def _():
            send_ref[slot] = chunks[q]


def project(at, hidden, hidden_te, cot, cot_te, ph, pc):
    shape = jax.ShapeDtypeStruct((2, 6, KX + KG, 128), F32)
    arrays = [hidden, hidden_te, cot, cot_te, ph, pc]
    any_spec = pl.BlockSpec(memory_space=pl.ANY)
    return pl.pallas_call(
        project_kernel,
        in_specs=[pl.BlockSpec(memory_space=pltpu.SMEM)] + [any_spec] * 6,
        out_specs=[vmem_spec()] * 2,
        out_shape=[shape, shape],
        scratch_shapes=[pltpu.VMEM(array.shape, BF16) for array in arrays]
        + [
            pltpu.VMEM((TOKS, KX, 256), F32),
            pltpu.VMEM((TOKS, KX, 128), F32),
            pltpu.VMEM((2048, 128), F32),
            pltpu.VMEM((1024, 128), F32),
            pltpu.VMEM((4, 6, KX + KG, 128), F32),
            pltpu.SemaphoreType.DMA((4 + 2 * TOKS,)),
        ],
        compiler_params=params(60),
        cost_estimate=pl.CostEstimate(flops=10**9, bytes_accessed=3 * 10**7, transcendentals=0),
        name="project",
    )(at, *arrays)


def feature_kernel(mine_ref, got_ref, lens_ref, train_ref, test_ref, send_ref, right, feat):
    for base, slots, out_ref in ((0, 4, train_ref), (4, 2, test_ref)):
        parts = TOKS // slots
        width = 128 // parts
        lens = lens_ref[base // 4 : base // 4 + 1, :]
        part = lax.broadcasted_iota(jnp.int32, (1, 128), 1) // width
        left = []
        for u in range(slots):
            at = base + u
            valid = lens > part * slots + u
            left.append(jnp.where(valid, mine_ref[at, 0:KX, :] + got_ref[at, 0:KX, :], 0.0))
            right[u] = mine_ref[at, KX : KX + KG, :] + got_ref[at, KX : KX + KG, :]
        for j in range(KG):
            acc = left[0] * right[0, j : j + 1, :]
            for u in range(1, slots):
                acc += left[u] * right[u, j : j + 1, :]
            feat[j * KX : (j + 1) * KX, :] = acc
        for k in range(K // 128):
            tall = feat[k * 128 : (k + 1) * 128, :].T
            block = tall[0:width]
            for p in range(1, parts):
                block += tall[p * width : (p + 1) * width]
            block = block.astype(BF16)
            out_ref[:, k * 128 : (k + 1) * 128] = block
            if base:
                continue
            group, off = divmod(k * 128, GROUP)
            for n, (i, j) in enumerate(TASKS):
                if i == group:
                    send_ref[n, :, off : off + 128] = block
                if j == group:
                    send_ref[n, :, GROUP + off : GROUP + off + 128] = block


def features(mine, got, lens):
    return pl.pallas_call(
        feature_kernel,
        in_specs=[vmem_spec()] * 3,
        out_specs=[vmem_spec()] * 3,
        out_shape=[
            jax.ShapeDtypeStruct((64, K), BF16),
            jax.ShapeDtypeStruct((32, K), BF16),
            jax.ShapeDtypeStruct((32, 64, 2 * GROUP), BF16),
        ],
        scratch_shapes=[pltpu.VMEM((4, KG, 128), F32), pltpu.VMEM((K, 128), F32)],
        compiler_params=params(40),
        name="features",
    )(mine, got, lens)


def gram_kernel(at_ref, rows_ref, send_ref, keep_ref, block, tail):
    left = rows_ref[:, 0:GROUP]
    right = rows_ref[:, GROUP : 2 * GROUP]
    tn = (((0,), (0,)), ((), ()))
    tail[...] = jnp.zeros((EXTRA - 128, 128), F32)

    @pl.when(at_ref[2] == 0)
    def _():
        block[...] = lax.dot_general(left, right, tn, preferred_element_type=F32)

    @pl.when(at_ref[2] == 1)
    def _():
        low = lax.dot_general(left, left, tn, preferred_element_type=F32)
        high = lax.dot_general(right, right, tn, preferred_element_type=F32)
        row = lax.broadcasted_iota(jnp.int32, (GROUP, GROUP), 0)
        col = lax.broadcasted_iota(jnp.int32, (GROUP, GROUP), 1)
        block[...] = jnp.where(row >= col, low, high)
        diag = jnp.sum(jnp.where(row == col, high, 0.0), axis=0, keepdims=True)
        tail[0:1, :] = diag[:, 0:128]
        tail[1:2, :] = diag[:, 128:256]
        tail[2:3, :] = diag[:, 0:128]
        tail[3:4, :] = diag[:, 128:256]
        diag = jnp.sum(jnp.where(row == col, low, 0.0), axis=0, keepdims=True)
        tail[4:5, :] = diag[:, 0:128]
        tail[5:6, :] = diag[:, 128:256]

    def fill(ref, slot, q):
        ref[slot, 0:64, :] = block[64 * q : 64 * q + 64, 0:128]
        ref[slot, 64:128, :] = block[64 * q : 64 * q + 64, 128:256]
        ref[slot, 128:EXTRA, :] = tail[...]

    for q in range(4):
        side, core = divmod(q, 2)
        slot = jnp.where(at_ref[1] == side, 0, 1)

        @pl.when(at_ref[0] == core)
        def _():
            fill(keep_ref, slot, q)

        @pl.when(at_ref[0] != core)
        def _():
            fill(send_ref, slot, q)


def gram_block(at, rows):
    shape = jax.ShapeDtypeStruct((2, EXTRA, 128), F32)
    return pl.pallas_call(
        gram_kernel,
        in_specs=[pl.BlockSpec(memory_space=pltpu.SMEM), vmem_spec()],
        out_specs=[vmem_spec()] * 2,
        out_shape=[shape, shape],
        scratch_shapes=[pltpu.VMEM((GROUP, GROUP), F32), pltpu.VMEM((EXTRA - 128, 128), F32)],
        compiler_params=params(40),
        name="gram_block",
    )(at, rows)


def split_kernel(want_low, mine_ref, got_ref, out_ref):
    total = mine_ref[...] + got_ref[...]
    high = total.astype(BF16).astype(F32)
    low = total - high
    if want_low:
        part = low.astype(BF16)
    else:
        row = lax.broadcasted_iota(jnp.int32, total.shape, 0)
        fine = jnp.logical_and(row >= 130, row < 134)
        part = jnp.where(fine, low, high).astype(BF16)
    for n in range(64):
        out_ref[n] = part


def split(mine, got, want_low):
    return pl.pallas_call(
        functools.partial(split_kernel, want_low),
        in_specs=[vmem_spec()] * 2,
        out_specs=vmem_spec(),
        out_shape=jax.ShapeDtypeStruct((64, EXTRA, 128), BF16),
        compiler_params=params(60),
        name="split_low" if want_low else "split_high",
    )(mine, got)


def unpack(core, own, other, out, trace_ref, fine_ref=None):
    @pl.when(core == 0)
    def _():
        unpack_parts((own, other), out, trace_ref, fine_ref)

    @pl.when(core == 1)
    def _():
        unpack_parts((other, own), out, trace_ref, fine_ref)

    return jnp.sum(trace_ref[0:1, :], axis=1, keepdims=True)


def unpack_parts(parts, out, trace_ref, fine_ref):
    row = lax.broadcasted_iota(jnp.int32, (GROUP, GROUP), 0)
    col = lax.broadcasted_iota(jnp.int32, (GROUP, GROUP), 1)
    trace = jnp.zeros((1, GROUP), F32)
    for n, (i, j) in enumerate(TASKS):
        pieces = []
        for q in range(4):
            h, c = divmod(q, 2)
            pieces.append(
                jnp.concatenate(
                    [parts[c][2 * n + h, 0:64, :], parts[c][2 * n + h, 64:128, :]], axis=1
                )
            )
        block = jnp.concatenate(pieces, axis=0)
        i0, j0 = i * GROUP, j * GROUP
        if n < N_OFF:
            out[i0 : i0 + GROUP, j0 : j0 + GROUP] = block
            out[j0 : j0 + GROUP, i0 : i0 + GROUP] = block.T
        else:
            wide = block.astype(F32)
            flipped = wide.T
            tail = parts[0][2 * n, 128:EXTRA, :].astype(F32)
            diag = jnp.concatenate([tail[0:1], tail[1:2]], axis=1)
            if fine_ref is not None:
                fine_ref[0:1, j0 : j0 + GROUP] = jnp.concatenate([tail[2:3], tail[3:4]], axis=1)
                fine_ref[0:1, i0 : i0 + GROUP] = jnp.concatenate([tail[4:5], tail[5:6]], axis=1)
            low = jnp.where(row >= col, wide, flipped)
            high = jnp.where(row < col, wide, jnp.where(row > col, flipped, diag))
            trace += jnp.sum(jnp.where(row == col, wide, 0.0), axis=0, keepdims=True) + diag
            out[i0 : i0 + GROUP, i0 : i0 + GROUP] = low.astype(BF16)
            out[j0 : j0 + GROUP, j0 : j0 + GROUP] = high.astype(BF16)
    trace_ref[0:1, :] = trace


def rows_dot(a, b):
    return jnp.sum(a * b, axis=1, keepdims=True)


BLOCKS = [slice(n * GROUP, (n + 1) * GROUP) for n in range(GROUPS)]


def product(high, low, p, y, gain):
    upper = [p[:, cols].astype(BF16) for cols in BLOCKS]
    lower = [(p[:, cols] - up.astype(F32)).astype(BF16) for cols, up in zip(BLOCKS, upper)]
    left = jnp.concatenate(upper, axis=1)
    both = jnp.concatenate([left, jnp.concatenate(lower, axis=1)], axis=0)
    total = jnp.zeros((64, GROUP), F32)
    for cols in BLOCKS:
        main = jnp.dot(both, high[:, cols], preferred_element_type=F32)
        rest = jnp.dot(left, low[:, cols], preferred_element_type=F32)
        value = (main[0:64] + main[64:128] + rest) * gain + 0.1 * p[:, cols]
        y[:, cols] = value
        total += value * p[:, cols]
    return jnp.sum(total, axis=1, keepdims=True)


def advance(high, low, x, r, p, y, gain, rr):
    py = product(high, low, p, y, gain)
    alpha = jnp.where(py > 0.0, rr / jnp.where(py > 0.0, py, 1.0), 0.0)
    new = jnp.zeros((64, GROUP), F32)
    xx = jnp.zeros((64, GROUP), F32)
    for cols in BLOCKS:
        xv = x[:, cols] + alpha * p[:, cols]
        rv = r[:, cols] - alpha * y[:, cols]
        x[:, cols] = xv
        r[:, cols] = rv
        xx += xv * xv
        new += rv * rv
    new = jnp.sum(new, axis=1, keepdims=True)
    beta = new / jnp.where(rr > 0.0, rr, 1.0)
    for cols in BLOCKS:
        p[:, cols] = r[:, cols] + beta * p[:, cols]
    return new, jnp.sum(xx, axis=1, keepdims=True)


def advance_start(high, fine, x, r, p, pb, y, gain, rr, rp):
    left = pb[...]
    py = jnp.zeros((64, GROUP), F32)
    for cols in BLOCKS:
        main = jnp.dot(left, high[:, cols], preferred_element_type=F32)
        step = p[:, cols]
        value = main * gain + (fine[0:1, cols] * gain + 0.1) * step
        y[:, cols] = value
        py += value * step
    py = jnp.sum(py, axis=1, keepdims=True)
    alpha = jnp.where(py > 0.0, rp / jnp.where(py > 0.0, py, 1.0), 0.0)
    new = jnp.zeros((64, GROUP), F32)
    for cols in BLOCKS:
        xv = x[:, cols] + alpha * p[:, cols]
        rv = r[:, cols] - alpha * y[:, cols]
        x[:, cols] = xv
        r[:, cols] = rv
        new += rv * rv
    new = jnp.sum(new, axis=1, keepdims=True)
    beta = new / jnp.where(rr > 0.0, rr, 1.0)
    rp = jnp.zeros((64, GROUP), F32)
    for cols in BLOCKS:
        rv = r[:, cols]
        step = (rv + beta * p[:, cols]).astype(BF16)
        pb[:, cols] = step
        wide = step.astype(F32)
        p[:, cols] = wide
        rp += rv * wide
    return new, jnp.sum(rp, axis=1, keepdims=True)


def scaled(f_ref):
    f = f_ref[...].astype(F32)
    top = jnp.max(jnp.abs(f), axis=1, keepdims=True)
    top = jnp.where(top > 0.0, top, 1.0)
    return f / top, top


def start_kernel(
    core_ref, own, other, f_ref, x0_ref, base_ref, trace_ref, gram, high, fine, x, r, p, pb, y, sem
):
    f, _ = scaled(f_ref)
    r[...] = f
    pb[...] = f.astype(BF16)
    p[...] = pb[...].astype(F32)
    x[...] = jnp.zeros_like(f)
    trace = unpack(core_ref[0], own, other, high, trace_ref, fine)
    gain = K / (trace + jnp.sum(fine[0:1, :], axis=1, keepdims=True))
    keep = pltpu.make_async_copy(high, gram.at[0], sem)
    keep.start()
    lax.fori_loop(
        0,
        START_STEPS,
        lambda _, state: advance_start(high, fine, x, r, p, pb, y, gain, *state),
        (rows_dot(f, f), rows_dot(f, p[...])),
    )
    x0 = x[...]
    x0_ref[...] = x0
    upper = x0.astype(BF16)
    both = jnp.concatenate([upper, (x0 - upper.astype(F32)).astype(BF16)], axis=0)
    for cols in BLOCKS:
        main = jnp.dot(both, high[:, cols], preferred_element_type=F32)
        base_ref[:, cols] = main[0:64] + main[64:128]
    keep.wait()


def solve_start(core, own, other, f):
    return pl.pallas_call(
        start_kernel,
        in_specs=[pl.BlockSpec(memory_space=pltpu.SMEM)] + [vmem_spec()] * 3,
        out_specs=[vmem_spec()] * 3 + [pl.BlockSpec(memory_space=pl.ANY)],
        out_shape=[
            jax.ShapeDtypeStruct((64, K), F32),
            jax.ShapeDtypeStruct((64, K), F32),
            jax.ShapeDtypeStruct((8, GROUP), F32),
            jax.ShapeDtypeStruct((SLABS, K, K), BF16),
        ],
        scratch_shapes=[
            pltpu.VMEM((K, K), BF16),
            pltpu.VMEM((8, K), F32),
            pltpu.VMEM((64, K), F32),
            pltpu.VMEM((64, K), F32),
            pltpu.VMEM((64, K), F32),
            pltpu.VMEM((64, K), BF16),
            pltpu.VMEM((64, K), F32),
            pltpu.SemaphoreType.DMA,
        ],
        cost_estimate=pl.CostEstimate(flops=START_FLOPS, bytes_accessed=10**7, transcendentals=0),
        compiler_params=params(18),
        name="solve_start",
    )(core, own, other, f)


def finish_kernel(
    core_ref,
    own,
    other,
    gram,
    f_ref,
    x0_ref,
    base_ref,
    trace_ref,
    w_ref,
    high,
    low,
    low_trace,
    x,
    r,
    p,
    y,
    sem,
):
    load = pltpu.make_async_copy(gram.at[0], high, sem)
    load.start()
    f, top = scaled(f_ref)
    trace = jnp.sum(trace_ref[0:1, :], axis=1, keepdims=True)
    trace = trace + unpack(core_ref[0], own, other, low, low_trace)
    gain = K / trace
    x0 = x0_ref[...]
    upper = x0.astype(BF16)
    for cols in BLOCKS:
        main = base_ref[:, cols] + jnp.dot(upper, low[:, cols], preferred_element_type=F32)
        y[:, cols] = main * gain + 0.1 * x0_ref[:, cols]
    ff = rows_dot(f, f)
    rest = f - y[...]
    rr = rows_dot(rest, rest)
    good = rr <= ff
    rr = jnp.where(good, rr, ff)
    first = jnp.where(good, x0, 0.0)
    rest = jnp.where(good, rest, f)
    x[...] = first
    r[...] = rest
    p[...] = rest
    load.wait()

    def excess(rr, xx):
        return jnp.max(rr - (0.1 * TOL) ** 2 * xx)

    def more(state):
        return jnp.logical_and(state[0] < MAX_STEPS, state[2] > 0.0)

    def body(state):
        step, rr, _ = state
        rr, xx = advance(high, low, x, r, p, y, gain, rr)
        return step + 1, rr, excess(rr, xx)

    lax.while_loop(more, body, (jnp.int32(0), rr, excess(rr, rows_dot(first, first))))
    w_ref[...] = (x[...] * (top * (COUNT * K / trace))).astype(BF16)


def solve_finish(core, own, other, high, f, x0, base, trace):
    return pl.pallas_call(
        finish_kernel,
        in_specs=[pl.BlockSpec(memory_space=pltpu.SMEM)] + [vmem_spec()] * 2
        + [pl.BlockSpec(memory_space=pl.ANY)]
        + [vmem_spec()] * 4,
        out_specs=vmem_spec(),
        out_shape=jax.ShapeDtypeStruct((64, K), BF16),
        scratch_shapes=[
            pltpu.VMEM((K, K), BF16),
            pltpu.VMEM((K, K), BF16),
            pltpu.VMEM((8, GROUP), F32),
            pltpu.VMEM((64, K), F32),
            pltpu.VMEM((64, K), F32),
            pltpu.VMEM((64, K), F32),
            pltpu.VMEM((64, K), F32),
            pltpu.SemaphoreType.DMA,
        ],
        cost_estimate=pl.CostEstimate(flops=FINISH_FLOPS, bytes_accessed=10**7, transcendentals=0),
        compiler_params=params(28),
        name="solve_finish",
    )(core, own, other, high, f, x0, base, trace)


def place_kernel(place_ref, *refs):
    out_ref = refs[-1]
    for me in range(4):

        @pl.when(2 * place_ref[1] + place_ref[0] == me)
        def _():
            for d in range(32):
                at = 64 * (d % 16) + 32 * (d // 16)
                out_ref[:, 128 * d : 128 * d + 128] = jnp.concatenate(
                    [refs[me ^ q][:, at : at + 32].astype(F32) for q in range(4)], axis=1
                )


def place(index, parts):
    return pl.pallas_call(
        place_kernel,
        in_specs=[pl.BlockSpec(memory_space=pltpu.SMEM)] + [vmem_spec()] * 4,
        out_specs=vmem_spec(),
        out_shape=jax.ShapeDtypeStruct((64, 4096), F32),
        compiler_params=params(40),
        name="place",
    )(index, *parts)


def fold(send, keep):
    recv = lax.ppermute(send, "proj", CORE_SWAP)
    return keep[0] + recv[0], lax.ppermute(keep[1] + recv[1], "proj", FAR_SWAP)


def exchange(chunks):
    return lax.all_to_all(
        chunks, ("dp", "proj"), 0, 0, axis_index_groups=SAME_CORE, tiled=True
    )


def per_device(
    train_hidden,
    train_cotangent,
    test_hidden,
    test_cotangent,
    proj_hidden,
    proj_cotangent,
    train_lengths,
    test_lengths,
):
    quarter = lax.axis_index("proj").astype(jnp.uint32)
    far, core = (quarter >> 1).astype(jnp.int32), (quarter & 1).astype(jnp.int32)
    task = lax.axis_index("dp")
    d = train_cotangent.shape[2]
    at = jnp.stack([core, far, (task >= N_OFF).astype(jnp.int32), core * 0])
    ph, pc = proj_hidden.T, proj_cotangent.T
    send, keep = project(
        at,
        jnp.transpose(train_hidden, (1, 2, 0)),
        jnp.transpose(test_hidden, (1, 2, 0)),
        train_cotangent.reshape(-1, d),
        test_cotangent.reshape(-1, d),
        ph,
        pc,
    )
    lens = jnp.stack(
        [
            jnp.tile(lax.dynamic_slice_in_dim(train_lengths, quarter * 64, 64), 2),
            jnp.tile(lax.dynamic_slice_in_dim(test_lengths, quarter * 32, 32), 4),
        ]
    )
    train, test, send = features(*fold(send, keep), lens)
    pairs = lax.all_gather(test, "dp", axis_index_groups=NEAR, axis=0, tiled=True)
    rows = lax.all_to_all(send, "dp", 0, 0, tiled=True).reshape(2048, 2 * GROUP)
    rows, pairs = lax.optimization_barrier((rows, pairs))
    tests = lax.all_gather(pairs, "dp", axis_index_groups=PLANES, axis=0, tiled=True)
    mine, got = fold(*gram_block(at, rows))
    high, low = split(mine, got, False), split(mine, got, True)
    high_own, low = lax.optimization_barrier((exchange(high), low))
    high_other = lax.ppermute(high_own, "proj", CORE_SWAP)
    low_own = exchange(low)
    x0, base, trace, gram = solve_start(at, high_own, high_other, train)
    low_own, x0 = lax.optimization_barrier((low_own, x0))
    low_other = lax.ppermute(low_own, "proj", CORE_SWAP)
    weighted = solve_finish(at, low_own, low_other, gram, train, x0, base, trace)
    weighted, tests = lax.optimization_barrier((weighted, tests))
    beyond = lax.ppermute(weighted, "proj", FAR_SWAP)
    tests_other = lax.ppermute(tests, "proj", CORE_SWAP)
    scale = 1.0 / math.sqrt(K)

    def scores(w, t):
        nt = (((1,), (1,)), ((), ()))
        return lax.dot_general(w, t, nt, preferred_element_type=F32) * scale

    near = scores(weighted, tests)
    beyond, near = lax.optimization_barrier((beyond, near))
    sent = jnp.concatenate([scores(beyond, tests), scores(beyond, tests_other)], axis=1)
    got = lax.ppermute(sent.astype(BF16), "proj", FAR_SWAP)
    return place(
        at,
        [near, scores(weighted, tests_other), got[:, 0:1024], got[:, 1024:]],
    )


def solution(mesh):
    in_specs = (
        P("dp", None, "proj"),
        P("dp", None, "proj"),
        P("dp", None, "proj"),
        P("dp", None, "proj"),
        P("proj", None),
        P("proj", None),
        P("dp"),
        P("dp"),
    )
    out_specs = P(("dp", "proj"), None)
    return jax.shard_map(
        per_device, mesh=mesh, in_specs=in_specs, out_specs=out_specs, check_vma=False
    )
```

```python
import functools
import math

import jax
import jax.numpy as jnp
import numpy as np
from jax import lax
from jax.experimental import pallas as pl
from jax.experimental.pallas import tpu as pltpu
from jax.sharding import PartitionSpec as P

KX = 32
KG = 64
K = 2048
TOKS = 8
COUNT = 8192
GROUP = 256
GROUPS = K // GROUP
EXTRA = 136
TOL = 2.0**-9
START_STEPS = 13
SLABS = 8
START_FLOPS = 10**9
FINISH_FLOPS = 10**9
MAX_STEPS = 8192

TASKS = [(i, j) for i in range(GROUPS) for j in range(i + 1, GROUPS)]
N_OFF = len(TASKS)
TASKS = TASKS + [(2 * k, 2 * k + 1) for k in range(GROUPS // 2)]

F32 = jnp.float32
BF16 = jnp.bfloat16
CORE_SWAP = [(0, 1), (1, 0), (2, 3), (3, 2)]
FAR_SWAP = [(0, 2), (2, 0), (1, 3), (3, 1)]
NEAR = [[i, i + 16] for i in range(16)]
PLANES = [[h * 16 + i for i in range(16)] for h in range(2)]
SAME_CORE = [[d * 4 + h * 2 + c for d in range(32) for h in range(2)] for c in range(2)]


def vmem_spec():
    return pl.BlockSpec(memory_space=pltpu.VMEM)


def params(mib):
    return pltpu.CompilerParams(vmem_limit_bytes=mib * 1024 * 1024)


def project_kernel(
    at_ref,
    h_ref,
    ht_ref,
    c_ref,
    ct_ref,
    ph_ref,
    pc_ref,
    send_ref,
    keep_ref,
    h,
    ht,
    c,
    ct,
    ph,
    pc,
    left,
    left_te,
    right,
    right_te,
    chunks,
    sems,
):
    def token(t):
        return (
            pltpu.make_async_copy(h_ref.at[t], h.at[t], sems.at[4 + t]),
            pltpu.make_async_copy(ht_ref.at[t], ht.at[t], sems.at[4 + TOKS + t]),
        )

    first = [
        pltpu.make_async_copy(src, dst, sems.at[n])
        for n, (src, dst) in enumerate([(pc_ref, pc), (c_ref, c), (ct_ref, ct), (ph_ref, ph)])
    ]
    for copy in first:
        copy.start()
    for t in range(TOKS):
        for copy in token(t):
            copy.start()

    nt = (((1,), (1,)), ((), ()))
    first[0].wait()
    for n, src, dst, slots, base in ((1, c, right, 4, 0), (2, ct, right_te, 2, 4)):
        first[n].wait()
        dst[:, 0:KG] = lax.dot_general(src[...], pc[...], nt, preferred_element_type=F32)
        examples = dst.shape[0] // TOKS
        parts = TOKS // slots
        width = examples // 4
        for u in range(slots):
            tall = [dst[pl.ds(p * slots + u, examples, stride=TOKS), :].T for p in range(parts)]
            for q in range(4):
                chunks[q, base + u, KX : KX + KG, :] = jnp.concatenate(
                    [piece[0:KG, width * q : width * (q + 1)] for piece in tall], axis=1
                )
    first[3].wait()

    def step(t, carry):
        for copy in token(t):
            copy.wait()
        left[t] = jnp.dot(ph[...], h[t], preferred_element_type=F32)
        left_te[t] = jnp.dot(ph[...], ht[t], preferred_element_type=F32)
        return carry

    lax.fori_loop(0, TOKS, step, 0)
    for src, slots, base in ((left, 4, 0), (left_te, 2, 4)):
        parts = TOKS // slots
        width = src.shape[2] // 4
        for u in range(slots):
            for q in range(4):
                chunks[q, base + u, 0:KX, :] = jnp.concatenate(
                    [src[p * slots + u, :, width * q : width * (q + 1)] for p in range(parts)],
                    axis=1,
                )
    for q in range(4):
        side, core = divmod(q, 2)
        slot = jnp.where(at_ref[1] == side, 0, 1)

        @pl.when(at_ref[0] == core)
        def _():
            keep_ref[slot] = chunks[q]

        @pl.when(at_ref[0] != core)
        def _():
            send_ref[slot] = chunks[q]


def project(at, hidden, hidden_te, cot, cot_te, ph, pc):
    shape = jax.ShapeDtypeStruct((2, 6, KX + KG, 128), F32)
    arrays = [hidden, hidden_te, cot, cot_te, ph, pc]
    any_spec = pl.BlockSpec(memory_space=pl.ANY)
    return pl.pallas_call(
        project_kernel,
        in_specs=[pl.BlockSpec(memory_space=pltpu.SMEM)] + [any_spec] * 6,
        out_specs=[vmem_spec()] * 2,
        out_shape=[shape, shape],
        scratch_shapes=[pltpu.VMEM(array.shape, BF16) for array in arrays]
        + [
            pltpu.VMEM((TOKS, KX, 256), F32),
            pltpu.VMEM((TOKS, KX, 128), F32),
            pltpu.VMEM((2048, 128), F32),
            pltpu.VMEM((1024, 128), F32),
            pltpu.VMEM((4, 6, KX + KG, 128), F32),
            pltpu.SemaphoreType.DMA((4 + 2 * TOKS,)),
        ],
        compiler_params=params(60),
        cost_estimate=pl.CostEstimate(flops=10**9, bytes_accessed=3 * 10**7, transcendentals=0),
        name="project",
    )(at, *arrays)


def feature_kernel(mine_ref, got_ref, lens_ref, train_ref, test_ref, send_ref, right, feat):
    for base, slots, out_ref in ((0, 4, train_ref), (4, 2, test_ref)):
        parts = TOKS // slots
        width = 128 // parts
        lens = lens_ref[base // 4 : base // 4 + 1, :]
        part = lax.broadcasted_iota(jnp.int32, (1, 128), 1) // width
        left = []
        for u in range(slots):
            at = base + u
            valid = lens > part * slots + u
            left.append(jnp.where(valid, mine_ref[at, 0:KX, :] + got_ref[at, 0:KX, :], 0.0))
            right[u] = mine_ref[at, KX : KX + KG, :] + got_ref[at, KX : KX + KG, :]
        for j in range(KG):
            acc = left[0] * right[0, j : j + 1, :]
            for u in range(1, slots):
                acc += left[u] * right[u, j : j + 1, :]
            feat[j * KX : (j + 1) * KX, :] = acc
        for k in range(K // 128):
            tall = feat[k * 128 : (k + 1) * 128, :].T
            block = tall[0:width]
            for p in range(1, parts):
                block += tall[p * width : (p + 1) * width]
            block = block.astype(BF16)
            out_ref[:, k * 128 : (k + 1) * 128] = block
            if base:
                continue
            group, off = divmod(k * 128, GROUP)
            for n, (i, j) in enumerate(TASKS):
                if i == group:
                    send_ref[n, :, off : off + 128] = block
                if j == group:
                    send_ref[n, :, GROUP + off : GROUP + off + 128] = block


def features(mine, got, lens):
    return pl.pallas_call(
        feature_kernel,
        in_specs=[vmem_spec()] * 3,
        out_specs=[vmem_spec()] * 3,
        out_shape=[
            jax.ShapeDtypeStruct((64, K), BF16),
            jax.ShapeDtypeStruct((32, K), BF16),
            jax.ShapeDtypeStruct((32, 64, 2 * GROUP), BF16),
        ],
        scratch_shapes=[pltpu.VMEM((4, KG, 128), F32), pltpu.VMEM((K, 128), F32)],
        compiler_params=params(40),
        name="features",
    )(mine, got, lens)


def gram_kernel(at_ref, rows_ref, send_ref, keep_ref, block, tail):
    left = rows_ref[:, 0:GROUP]
    right = rows_ref[:, GROUP : 2 * GROUP]
    tn = (((0,), (0,)), ((), ()))
    tail[...] = jnp.zeros((EXTRA - 128, 128), F32)

    @pl.when(at_ref[2] == 0)
    def _():
        block[...] = lax.dot_general(left, right, tn, preferred_element_type=F32)

    @pl.when(at_ref[2] == 1)
    def _():
        low = lax.dot_general(left, left, tn, preferred_element_type=F32)
        high = lax.dot_general(right, right, tn, preferred_element_type=F32)
        row = lax.broadcasted_iota(jnp.int32, (GROUP, GROUP), 0)
        col = lax.broadcasted_iota(jnp.int32, (GROUP, GROUP), 1)
        block[...] = jnp.where(row >= col, low, high)
        diag = jnp.sum(jnp.where(row == col, high, 0.0), axis=0, keepdims=True)
        tail[0:1, :] = diag[:, 0:128]
        tail[1:2, :] = diag[:, 128:256]
        tail[2:3, :] = diag[:, 0:128]
        tail[3:4, :] = diag[:, 128:256]
        diag = jnp.sum(jnp.where(row == col, low, 0.0), axis=0, keepdims=True)
        tail[4:5, :] = diag[:, 0:128]
        tail[5:6, :] = diag[:, 128:256]

    def fill(ref, slot, q):
        ref[slot, 0:64, :] = block[64 * q : 64 * q + 64, 0:128]
        ref[slot, 64:128, :] = block[64 * q : 64 * q + 64, 128:256]
        ref[slot, 128:EXTRA, :] = tail[...]

    for q in range(4):
        side, core = divmod(q, 2)
        slot = jnp.where(at_ref[1] == side, 0, 1)

        @pl.when(at_ref[0] == core)
        def _():
            fill(keep_ref, slot, q)

        @pl.when(at_ref[0] != core)
        def _():
            fill(send_ref, slot, q)


def gram_block(at, rows):
    shape = jax.ShapeDtypeStruct((2, EXTRA, 128), F32)
    return pl.pallas_call(
        gram_kernel,
        in_specs=[pl.BlockSpec(memory_space=pltpu.SMEM), vmem_spec()],
        out_specs=[vmem_spec()] * 2,
        out_shape=[shape, shape],
        scratch_shapes=[pltpu.VMEM((GROUP, GROUP), F32), pltpu.VMEM((EXTRA - 128, 128), F32)],
        compiler_params=params(40),
        name="gram_block",
    )(at, rows)


def split_kernel(want_low, mine_ref, got_ref, out_ref):
    total = mine_ref[...] + got_ref[...]
    high = total.astype(BF16).astype(F32)
    low = total - high
    if want_low:
        part = low.astype(BF16)
    else:
        row = lax.broadcasted_iota(jnp.int32, total.shape, 0)
        fine = jnp.logical_and(row >= 130, row < 134)
        part = jnp.where(fine, low, high).astype(BF16)
    for n in range(64):
        out_ref[n] = part


def split(mine, got, want_low):
    return pl.pallas_call(
        functools.partial(split_kernel, want_low),
        in_specs=[vmem_spec()] * 2,
        out_specs=vmem_spec(),
        out_shape=jax.ShapeDtypeStruct((64, EXTRA, 128), BF16),
        compiler_params=params(60),
        name="split_low" if want_low else "split_high",
    )(mine, got)


def unpack(core, own, other, out, trace_ref, fine_ref=None):
    @pl.when(core == 0)
    def _():
        unpack_parts((own, other), out, trace_ref, fine_ref)

    @pl.when(core == 1)
    def _():
        unpack_parts((other, own), out, trace_ref, fine_ref)

    return jnp.sum(trace_ref[0:1, :], axis=1, keepdims=True)


def unpack_parts(parts, out, trace_ref, fine_ref):
    row = lax.broadcasted_iota(jnp.int32, (GROUP, GROUP), 0)
    col = lax.broadcasted_iota(jnp.int32, (GROUP, GROUP), 1)
    trace = jnp.zeros((1, GROUP), F32)
    for n, (i, j) in enumerate(TASKS):
        pieces = []
        for q in range(4):
            h, c = divmod(q, 2)
            pieces.append(
                jnp.concatenate(
                    [parts[c][2 * n + h, 0:64, :], parts[c][2 * n + h, 64:128, :]], axis=1
                )
            )
        block = jnp.concatenate(pieces, axis=0)
        i0, j0 = i * GROUP, j * GROUP
        if n < N_OFF:
            out[i0 : i0 + GROUP, j0 : j0 + GROUP] = block
            out[j0 : j0 + GROUP, i0 : i0 + GROUP] = block.T
        else:
            wide = block.astype(F32)
            flipped = wide.T
            tail = parts[0][2 * n, 128:EXTRA, :].astype(F32)
            diag = jnp.concatenate([tail[0:1], tail[1:2]], axis=1)
            if fine_ref is not None:
                fine_ref[0:1, j0 : j0 + GROUP] = jnp.concatenate([tail[2:3], tail[3:4]], axis=1)
                fine_ref[0:1, i0 : i0 + GROUP] = jnp.concatenate([tail[4:5], tail[5:6]], axis=1)
            low = jnp.where(row >= col, wide, flipped)
            high = jnp.where(row < col, wide, jnp.where(row > col, flipped, diag))
            trace += jnp.sum(jnp.where(row == col, wide, 0.0), axis=0, keepdims=True) + diag
            out[i0 : i0 + GROUP, i0 : i0 + GROUP] = low.astype(BF16)
            out[j0 : j0 + GROUP, j0 : j0 + GROUP] = high.astype(BF16)
    trace_ref[0:1, :] = trace


def rows_dot(a, b):
    return jnp.sum(a * b, axis=1, keepdims=True)


BLOCKS = [slice(n * GROUP, (n + 1) * GROUP) for n in range(GROUPS)]


def product(high, low, p, y, gain):
    upper = [p[:, cols].astype(BF16) for cols in BLOCKS]
    lower = [(p[:, cols] - up.astype(F32)).astype(BF16) for cols, up in zip(BLOCKS, upper)]
    left = jnp.concatenate(upper, axis=1)
    both = jnp.concatenate([left, jnp.concatenate(lower, axis=1)], axis=0)
    total = jnp.zeros((64, GROUP), F32)
    for cols in BLOCKS:
        main = jnp.dot(both, high[:, cols], preferred_element_type=F32)
        rest = jnp.dot(left, low[:, cols], preferred_element_type=F32)
        value = (main[0:64] + main[64:128] + rest) * gain + 0.1 * p[:, cols]
        y[:, cols] = value
        total += value * p[:, cols]
    return jnp.sum(total, axis=1, keepdims=True)


def advance(high, low, x, r, p, y, gain, rr):
    py = product(high, low, p, y, gain)
    alpha = jnp.where(py > 0.0, rr / jnp.where(py > 0.0, py, 1.0), 0.0)
    new = jnp.zeros((64, GROUP), F32)
    xx = jnp.zeros((64, GROUP), F32)
    for cols in BLOCKS:
        xv = x[:, cols] + alpha * p[:, cols]
        rv = r[:, cols] - alpha * y[:, cols]
        x[:, cols] = xv
        r[:, cols] = rv
        xx += xv * xv
        new += rv * rv
    new = jnp.sum(new, axis=1, keepdims=True)
    beta = new / jnp.where(rr > 0.0, rr, 1.0)
    for cols in BLOCKS:
        p[:, cols] = r[:, cols] + beta * p[:, cols]
    return new, jnp.sum(xx, axis=1, keepdims=True)


def advance_start(high, fine, x, r, p, pb, y, gain, rr, rp):
    left = pb[...]
    py = jnp.zeros((64, GROUP), F32)
    for cols in BLOCKS:
        main = jnp.dot(left, high[:, cols], preferred_element_type=F32)
        step = p[:, cols]
        value = main * gain + (fine[0:1, cols] * gain + 0.1) * step
        y[:, cols] = value
        py += value * step
    py = jnp.sum(py, axis=1, keepdims=True)
    alpha = jnp.where(py > 0.0, rp / jnp.where(py > 0.0, py, 1.0), 0.0)
    new = jnp.zeros((64, GROUP), F32)
    for cols in BLOCKS:
        xv = x[:, cols] + alpha * p[:, cols]
        rv = r[:, cols] - alpha * y[:, cols]
        x[:, cols] = xv
        r[:, cols] = rv
        new += rv * rv
    new = jnp.sum(new, axis=1, keepdims=True)
    beta = new / jnp.where(rr > 0.0, rr, 1.0)
    rp = jnp.zeros((64, GROUP), F32)
    for cols in BLOCKS:
        rv = r[:, cols]
        step = (rv + beta * p[:, cols]).astype(BF16)
        pb[:, cols] = step
        wide = step.astype(F32)
        p[:, cols] = wide
        rp += rv * wide
    return new, jnp.sum(rp, axis=1, keepdims=True)


def scaled(f_ref):
    f = f_ref[...].astype(F32)
    top = jnp.max(jnp.abs(f), axis=1, keepdims=True)
    top = jnp.where(top > 0.0, top, 1.0)
    return f / top, top


def start_kernel(
    core_ref, own, other, f_ref, x0_ref, base_ref, trace_ref, gram, high, fine, x, r, p, pb, y, sem
):
    f, _ = scaled(f_ref)
    r[...] = f
    pb[...] = f.astype(BF16)
    p[...] = pb[...].astype(F32)
    x[...] = jnp.zeros_like(f)
    trace = unpack(core_ref[0], own, other, high, trace_ref, fine)
    gain = K / (trace + jnp.sum(fine[0:1, :], axis=1, keepdims=True))
    keep = pltpu.make_async_copy(high, gram.at[0], sem)
    keep.start()
    lax.fori_loop(
        0,
        START_STEPS,
        lambda _, state: advance_start(high, fine, x, r, p, pb, y, gain, *state),
        (rows_dot(f, f), rows_dot(f, p[...])),
    )
    x0 = x[...]
    x0_ref[...] = x0
    upper = x0.astype(BF16)
    both = jnp.concatenate([upper, (x0 - upper.astype(F32)).astype(BF16)], axis=0)
    for cols in BLOCKS:
        main = jnp.dot(both, high[:, cols], preferred_element_type=F32)
        base_ref[:, cols] = main[0:64] + main[64:128]
    keep.wait()


def solve_start(core, own, other, f):
    return pl.pallas_call(
        start_kernel,
        in_specs=[pl.BlockSpec(memory_space=pltpu.SMEM)] + [vmem_spec()] * 3,
        out_specs=[vmem_spec()] * 3 + [pl.BlockSpec(memory_space=pl.ANY)],
        out_shape=[
            jax.ShapeDtypeStruct((64, K), F32),
            jax.ShapeDtypeStruct((64, K), F32),
            jax.ShapeDtypeStruct((8, GROUP), F32),
            jax.ShapeDtypeStruct((SLABS, K, K), BF16),
        ],
        scratch_shapes=[
            pltpu.VMEM((K, K), BF16),
            pltpu.VMEM((8, K), F32),
            pltpu.VMEM((64, K), F32),
            pltpu.VMEM((64, K), F32),
            pltpu.VMEM((64, K), F32),
            pltpu.VMEM((64, K), BF16),
            pltpu.VMEM((64, K), F32),
            pltpu.SemaphoreType.DMA,
        ],
        cost_estimate=pl.CostEstimate(flops=START_FLOPS, bytes_accessed=10**7, transcendentals=0),
        compiler_params=params(18),
        name="solve_start",
    )(core, own, other, f)


def finish_kernel(
    core_ref,
    own,
    other,
    gram,
    f_ref,
    x0_ref,
    base_ref,
    trace_ref,
    w_ref,
    high,
    low,
    low_trace,
    x,
    r,
    p,
    y,
    sem,
):
    load = pltpu.make_async_copy(gram.at[0], high, sem)
    load.start()
    f, top = scaled(f_ref)
    trace = jnp.sum(trace_ref[0:1, :], axis=1, keepdims=True)
    trace = trace + unpack(core_ref[0], own, other, low, low_trace)
    gain = K / trace
    x0 = x0_ref[...]
    upper = x0.astype(BF16)
    for cols in BLOCKS:
        main = base_ref[:, cols] + jnp.dot(upper, low[:, cols], preferred_element_type=F32)
        y[:, cols] = main * gain + 0.1 * x0_ref[:, cols]
    ff = rows_dot(f, f)
    rest = f - y[...]
    rr = rows_dot(rest, rest)
    good = rr <= ff
    rr = jnp.where(good, rr, ff)
    first = jnp.where(good, x0, 0.0)
    rest = jnp.where(good, rest, f)
    x[...] = first
    r[...] = rest
    p[...] = rest
    load.wait()

    def excess(rr, xx):
        return jnp.max(rr - (0.1 * TOL) ** 2 * xx)

    def more(state):
        return jnp.logical_and(state[0] < MAX_STEPS, state[2] > 0.0)

    def body(state):
        step, rr, _ = state
        rr, xx = advance(high, low, x, r, p, y, gain, rr)
        return step + 1, rr, excess(rr, xx)

    lax.while_loop(more, body, (jnp.int32(0), rr, excess(rr, rows_dot(first, first))))
    w_ref[...] = (x[...] * (top * (COUNT * K / trace))).astype(BF16)


def solve_finish(core, own, other, high, f, x0, base, trace):
    return pl.pallas_call(
        finish_kernel,
        in_specs=[pl.BlockSpec(memory_space=pltpu.SMEM)] + [vmem_spec()] * 2
        + [pl.BlockSpec(memory_space=pl.ANY)]
        + [vmem_spec()] * 4,
        out_specs=vmem_spec(),
        out_shape=jax.ShapeDtypeStruct((64, K), BF16),
        scratch_shapes=[
            pltpu.VMEM((K, K), BF16),
            pltpu.VMEM((K, K), BF16),
            pltpu.VMEM((8, GROUP), F32),
            pltpu.VMEM((64, K), F32),
            pltpu.VMEM((64, K), F32),
            pltpu.VMEM((64, K), F32),
            pltpu.VMEM((64, K), F32),
            pltpu.SemaphoreType.DMA,
        ],
        cost_estimate=pl.CostEstimate(flops=FINISH_FLOPS, bytes_accessed=10**7, transcendentals=0),
        compiler_params=params(28),
        name="solve_finish",
    )(core, own, other, high, f, x0, base, trace)


def place_kernel(place_ref, *refs):
    out_ref = refs[-1]
    for me in range(4):

        @pl.when(2 * place_ref[1] + place_ref[0] == me)
        def _():
            for d in range(32):
                at = 64 * (d % 16) + 32 * (d // 16)
                out_ref[:, 128 * d : 128 * d + 128] = jnp.concatenate(
                    [refs[me ^ q][:, at : at + 32].astype(F32) for q in range(4)], axis=1
                )


def place(index, parts):
    return pl.pallas_call(
        place_kernel,
        in_specs=[pl.BlockSpec(memory_space=pltpu.SMEM)] + [vmem_spec()] * 4,
        out_specs=vmem_spec(),
        out_shape=jax.ShapeDtypeStruct((64, 4096), F32),
        compiler_params=params(40),
        name="place",
    )(index, *parts)


def fold(send, keep):
    recv = lax.ppermute(send, "proj", CORE_SWAP)
    return keep[0] + recv[0], lax.ppermute(keep[1] + recv[1], "proj", FAR_SWAP)


def exchange(chunks):
    return lax.all_to_all(
        chunks, ("dp", "proj"), 0, 0, axis_index_groups=SAME_CORE, tiled=True
    )


def per_device(
    train_hidden,
    train_cotangent,
    test_hidden,
    test_cotangent,
    proj_hidden,
    proj_cotangent,
    train_lengths,
    test_lengths,
):
    quarter = lax.axis_index("proj").astype(jnp.uint32)
    far, core = (quarter >> 1).astype(jnp.int32), (quarter & 1).astype(jnp.int32)
    task = lax.axis_index("dp")
    d = train_cotangent.shape[2]
    at = jnp.stack([core, far, (task >= N_OFF).astype(jnp.int32), core * 0])
    ph, pc = proj_hidden.T, proj_cotangent.T
    send, keep = project(
        at,
        jnp.transpose(train_hidden, (1, 2, 0)),
        jnp.transpose(test_hidden, (1, 2, 0)),
        train_cotangent.reshape(-1, d),
        test_cotangent.reshape(-1, d),
        ph,
        pc,
    )
    lens = jnp.stack(
        [
            jnp.tile(lax.dynamic_slice_in_dim(train_lengths, quarter * 64, 64), 2),
            jnp.tile(lax.dynamic_slice_in_dim(test_lengths, quarter * 32, 32), 4),
        ]
    )
    train, test, send = features(*fold(send, keep), lens)
    pairs = lax.all_gather(test, "dp", axis_index_groups=NEAR, axis=0, tiled=True)
    rows = lax.all_to_all(send, "dp", 0, 0, tiled=True).reshape(2048, 2 * GROUP)
    rows, pairs = lax.optimization_barrier((rows, pairs))
    tests = lax.all_gather(pairs, "dp", axis_index_groups=PLANES, axis=0, tiled=True)
    mine, got = fold(*gram_block(at, rows))
    high, low = split(mine, got, False), split(mine, got, True)
    high_own, low = lax.optimization_barrier((exchange(high), low))
    high_other = lax.ppermute(high_own, "proj", CORE_SWAP)
    low_own = exchange(low)
    x0, base, trace, gram = solve_start(at, high_own, high_other, train)
    low_own, x0 = lax.optimization_barrier((low_own, x0))
    low_other = lax.ppermute(low_own, "proj", CORE_SWAP)
    weighted = solve_finish(at, low_own, low_other, gram, train, x0, base, trace)
    weighted, tests = lax.optimization_barrier((weighted, tests))
    beyond = lax.ppermute(weighted, "proj", FAR_SWAP)
    tests_other = lax.ppermute(tests, "proj", CORE_SWAP)
    scale = 1.0 / math.sqrt(K)

    def scores(w, t):
        nt = (((1,), (1,)), ((), ()))
        return lax.dot_general(w, t, nt, preferred_element_type=F32) * scale

    near = scores(weighted, tests)
    beyond, near = lax.optimization_barrier((beyond, near))
    sent = jnp.concatenate([scores(beyond, tests), scores(beyond, tests_other)], axis=1)
    got = lax.ppermute(sent.astype(BF16), "proj", FAR_SWAP)
    return place(
        at,
        [near, scores(weighted, tests_other), got[:, 0:1024], got[:, 1024:]],
    )


def solution(mesh):
    in_specs = (
        P("dp", None, "proj"),
        P("dp", None, "proj"),
        P("dp", None, "proj"),
        P("dp", None, "proj"),
        P("proj", None),
        P("proj", None),
        P("dp"),
        P("dp"),
    )
    out_specs = P(("dp", "proj"), None)
    return jax.shard_map(
        per_device, mesh=mesh, in_specs=in_specs, out_specs=out_specs, check_vma=False
    )
```
